32 devices in a mesh: dp: 8 (over z, core), expert: 4 (over y, x).
Axes of the slice: x: 2, y: 2, z: 4, core: 2. Of those that a mesh axis runs over, the one named last changes fastest.
Arguments:
- tokens: bfloat16 [8192, 2048], P(('dp', 'expert')), parts along dimension 0, may hold values from -6 to 6
- routes: int32 [8192, 2], P(('dp', 'expert')), parts along dimension 0, may hold values from 0 to 3, all different within a row; in each aligned block of 256 rows (0 to 255, 256 to 511, ...) at most 256 rows name the same one
- gate_values: bfloat16 [8192, 2], P(('dp', 'expert')), parts along dimension 0, may hold values from 0.099609375 to 1
- weight_in: bfloat16 [4, 2048, 1536], P('expert'), may hold values from -0.125 to 0.125
- weight_out: bfloat16 [4, 768, 2048], P('expert'), may hold values from -0.21875 to 0.21875
Outputs:
- mixed: bfloat16 [8192, 2048], P(('dp', 'expert')), parts along dimension 0
The draws below stay inside these ranges and needn't reach their ends.
There are 8 independent parts, one for each index of `dp`. The reference program is written for one: setup_inputs(seed, part) draws one part's arguments, and reference() takes and returns one part's arrays. A program takes and returns all parts, laid end to end along the dimension named above; an argument that names none is the same for every part. Nothing has to cross between parts.
Inputs may be any that keep to these rules, and one draw needn't show every extreme that they name: `routes`: each row names 2 different experts. In each aligned block of 256 rows (the rows of one device) no expert is named by more than 256 rows, a bound that some block reaches.
All inputs are finite; a program needn't handle non-finite values.
Results may differ from the reference program's by a relative error of at most 0.012.
Values may be sent and summed in bfloat16 or wider, within the bound.
A program may use at most 128 MiB of HBM per device.

```python
import math
import jax
import jax.numpy as jnp
import numpy as np
from jax import lax

D = 2048
FF = 768
TOP = 2
TOK_DEV = 256
EXPERTS = 4
TOKENS = 1024
MOST_SRC = 256


def block_levels(rng, shape, pieces, least, largest):
    loudness = 1.0
    for axis_at, blocks in pieces:
        draws = jax.random.uniform(jax.random.fold_in(jax.random.fold_in(rng, 6), axis_at), (blocks,), jnp.float32, least / len(pieces), largest / len(pieces))
        loudness = loudness * jnp.repeat(jnp.exp(draws), shape[axis_at] // blocks).reshape((-1,) + (1,) * (len(shape) - 1 - axis_at))
    return loudness


def shared_out(own_key, own, number, rows, count, top, reach, slope):
    sequence = jax.random.permutation(own_key, count)
    heavy_load, usual = portions_of(count, rows * top, reach, slope, True), portions_of(count, rows * top, reach, slope, False)
    places = jnp.arange(count)

    def named(tallies, offset_by):
        used = int((tallies > 0).sum())
        fixed = max(1, used // 4)
        shifted = fixed + (places - fixed + offset_by * (used - fixed)) % max(1, count - fixed)
        return jnp.zeros((count,), jnp.int32).at[sequence[jnp.where(places < fixed, places, shifted)]].set(jnp.asarray(tallies, jnp.int32))

    tallies = jnp.where(number % 4 == 0, named(heavy_load, number // 4), named(usual, number - number // 4 - 1))
    mixed = jax.random.permutation(jax.random.fold_in(own, 3), count)
    donor, taker = mixed[0:count // 2 * 2:2], mixed[1:count // 2 * 2:2]
    slack = jnp.minimum(tallies[donor] - 1, reach - tallies[taker]) // 2
    slack = jnp.where((donor == sequence[0]) | (taker == sequence[0]) | (tallies[taker] == 0), 0, jnp.maximum(slack, 0))
    shifted = jax.random.randint(jax.random.fold_in(own, 4), (count // 2,), 0, 1 << 20) % (slack + 1)
    tallies = tallies.at[donor].add(-shifted).at[taker].add(shifted)
    items = jnp.searchsorted(jnp.cumsum(tallies), jnp.arange(rows * top), side="right").astype(jnp.int32)
    grid = items.reshape(top, rows).T
    grid = grid[jax.random.permutation(jax.random.fold_in(own, 1), rows)]
    offset_by = jax.random.randint(jax.random.fold_in(own, 2), (rows, 1), 0, top)
    return jnp.take_along_axis(grid, (jnp.arange(top)[None, :] + offset_by) % top, axis=1)


def portions_of(number_of, total, limit, skew, full):
    weights = [(1 << 20) // math.isqrt(grade ** skew) + 1 for grade in range(1, number_of + 1)]
    largest = limit if full else min(limit, max(-(-total // number_of), total * weights[0] // sum(weights)))
    least = 1 if total - largest >= number_of - 1 else 0
    given, spare = [largest] + [least] * (number_of - 1), total - largest - least * (number_of - 1)
    while spare > 0:
        free = [i for i in range(1, number_of) if given[i] < largest] or [i for i in range(1, number_of) if given[i] < limit]
        whole, remaining = sum([weights[i] for i in free]), spare
        for i in free:
            addition = min(limit - given[i], max(1, remaining * weights[i] // whole), spare)
            given[i] = given[i] + addition
            spare = spare - addition
    return np.array(given)


def scatter_about(rng, extent, spread, most, shards=(), kind=jnp.bfloat16):
    result = spread * jax.random.normal(rng, extent, jnp.float32)
    if shards:
        result = result * block_levels(rng, extent, shards, -0.22, 0.18)
    return jnp.clip(result, -most, most).astype(kind)


def setup_inputs(seed: int = 0, part: int = 0) -> dict:
    streams_of = jax.random.split(jax.random.key(seed), 6)
    part_splits = jax.random.split(jax.random.fold_in(streams_of[5], part), 6)
    tokens = scatter_about(part_splits[0], (TOKENS, D), 1.0, 6.0, ((0, 4),))
    routes_keys = jax.random.split(jax.random.fold_in(part_splits[1], 1), TOKENS // TOK_DEV)
    routes_turns = jax.random.permutation(jax.random.fold_in(part_splits[1], 3), TOKENS // TOK_DEV)
    routes = jax.vmap(lambda own, number: shared_out(jax.random.fold_in(part_splits[1], 2), own, number, TOK_DEV, EXPERTS, TOP, MOST_SRC, 1))(routes_keys, routes_turns).reshape((TOKENS, TOP))
    gate_values = jnp.clip(0.099609375 + 0.9003906 * jax.random.uniform(part_splits[2], (TOKENS, TOP), jnp.float32) ** block_levels(part_splits[2], (TOKENS, TOP), ((0, 4),), -0.2, 0.2), 0.099609375, 1.0).astype(jnp.bfloat16)
    weight_in = scatter_about(streams_of[3], (EXPERTS, D, 2 * FF), D ** -0.5, 0.125, ((0, 4),))
    weight_out = scatter_about(streams_of[4], (EXPERTS, FF, D), FF ** -0.5, 0.21875, ((0, 4),))
    return dict(tokens=tokens, routes=routes, gate_values=gate_values, weight_in=weight_in, weight_out=weight_out)


def reference(tokens, routes, gate_values, weight_in, weight_out):
    gates_wide = gate_values.astype(jnp.float32)

    def one_expert(summed, items):
        w_first, w_second, expert_id = items
        combine = jnp.sum(jnp.where(routes == expert_id, gates_wide, 0.0), axis=1)
        projected = jnp.dot(tokens, w_first, preferred_element_type=jnp.float32)
        hidden = (jax.nn.silu(projected[:, :FF]) * projected[:, FF:]).astype(jnp.bfloat16)
        expert_out = jnp.dot(hidden, w_second, preferred_element_type=jnp.float32)
        contribution = (expert_out * combine[:, None]).astype(jnp.bfloat16)
        return summed + contribution.astype(jnp.float32), None

    start = jnp.zeros((TOKENS, D), jnp.float32)
    summed, unused = lax.scan(one_expert, start, (weight_in, weight_out, jnp.arange(EXPERTS, dtype=jnp.int32)))
    return summed.astype(jnp.bfloat16)
```

```python
import jax
import jax.numpy as jnp
from jax import lax
from jax.experimental import pallas as pl
from jax.experimental.pallas import tpu as pltpu
from jax.sharding import PartitionSpec as P

MESH = pl.DeviceIdType.MESH


def square_kernel(
    routes_ref, gates_ref, tokens_ref, w_in_ref, w_out_ref, out_ref,
    w1, w2, own, buf_x, buf_y, buf_d, comb_own, comb_x, comb_y, comb_d,
    c_own, c_x, c_y, c_d, got_x, got_y, via_y, via_x, hidden,
    local_sem, send_sem, recv_sem,
):
    me = lax.axis_index("expert")
    x_dev = me + 1 - 2 * (me % 2)
    y_dev = (me + 2) % 4
    rows, width = own.shape
    half = rows // 2
    units = w2.shape[0]
    first, second = 0, half
    piece = half // 4

    barrier = pltpu.get_barrier_semaphore()
    for dev in (x_dev, y_dev):
        pl.semaphore_signal(barrier, inc=1, device_id={"expert": dev}, device_id_type=MESH)

    load_w1 = pltpu.make_async_copy(w_in_ref, w1, local_sem.at[0])
    load_w2 = pltpu.make_async_copy(w_out_ref, w2, local_sem.at[1])
    load_own = pltpu.make_async_copy(tokens_ref, own, local_sem.at[2])
    load_own.start()
    load_w1.start()
    load_w2.start()

    experts = lax.broadcasted_iota(jnp.int32, comb_own.shape, 0)
    combined = jnp.zeros(comb_own.shape, jnp.float32)
    for j in range(routes_ref.shape[0]):
        combined += jnp.where(
            experts == routes_ref[j : j + 1, :], gates_ref[j : j + 1, :].astype(jnp.float32), 0.0
        )
    comb_own[...] = combined.astype(jnp.bfloat16)

    pl.semaphore_wait(barrier, 2)

    count = [0]
    sent = []

    def send(src, dst, dev):
        k = count[0]
        count[0] += 1
        copy = pltpu.make_async_remote_copy(
            src_ref=src,
            dst_ref=dst,
            send_sem=send_sem.at[k],
            recv_sem=recv_sem.at[k],
            device_id={"expert": dev},
            device_id_type=MESH,
        )
        copy.start()
        sent.append(copy)
        return copy

    def part(ref, start, size):
        return ref.at[pl.ds(start, size)]

    tok_x0 = send(part(tokens_ref, first, half), part(buf_x, first, half), x_dev)
    tok_y1 = send(part(tokens_ref, second, half), part(buf_y, second, half), y_dev)
    com_x = send(comb_own, comb_x, x_dev)
    com_y = send(comb_own, comb_y, y_dev)
    tok_x1 = send(part(tokens_ref, second, half), part(buf_x, second, half), x_dev)
    tok_y0 = send(part(tokens_ref, first, half), part(buf_y, first, half), y_dev)

    tile = 256

    def compute(src, comb, dst, start):
        def first_step(j, carry):
            cols = pl.multiple_of(j * tile, tile)
            x = src[pl.ds(start, half), :]
            gate = jnp.dot(x, w1[:, pl.ds(cols, tile)], preferred_element_type=jnp.float32)
            up = jnp.dot(x, w1[:, pl.ds(cols + units, tile)], preferred_element_type=jnp.float32)
            hidden[:, pl.ds(cols, tile)] = (gate / (1.0 + jnp.exp(-gate)) * up).astype(jnp.bfloat16)
            return carry

        lax.fori_loop(0, units // tile, first_step, 0)
        pick = (lax.broadcasted_iota(jnp.int32, (comb.shape[0], 128), 0) == me).astype(jnp.bfloat16)
        weight = lax.dot_general(
            comb[:, pl.ds(start, half)], pick, (((0,), (0,)), ((), ())),
            preferred_element_type=jnp.float32,
        )[:, :1]

        def second_step(j, carry):
            cols = pl.multiple_of(j * 512, 512)
            got = jnp.dot(
                hidden[...], w2[:, pl.ds(cols, 512)], preferred_element_type=jnp.float32
            )
            dst[pl.ds(start, half), pl.ds(cols, 512)] = (got * weight).astype(jnp.bfloat16)
            return carry

        lax.fori_loop(0, width // 512, second_step, 0)

    load_own.wait()
    load_w1.wait()
    load_w2.wait()
    compute(own, comb_own, c_own, first)
    compute(own, comb_own, c_own, second)

    com_x.wait_recv()
    com_y.wait_recv()
    com_d = send(comb_x, comb_d, y_dev)
    tok_x0.wait_recv()
    tok_d0 = send(part(buf_x, first, half), part(buf_d, first, half), y_dev)
    tok_y1.wait_recv()
    tok_d1 = send(part(buf_y, second, half), part(buf_d, second, half), x_dev)
    compute(buf_x, comb_x, c_x, first)
    compute(buf_y, comb_y, c_y, second)

    tok_x1.wait_recv()
    compute(buf_x, comb_x, c_x, second)
    straight = []
    straight.append(send(part(c_x, second, half // 2), part(got_x, second, half // 2), x_dev))
    tok_y0.wait_recv()
    compute(buf_y, comb_y, c_y, first)
    straight.append(send(part(c_y, first, half // 2), part(got_y, first, half // 2), y_dev))

    com_d.wait_recv()
    tok_d0.wait_recv()
    compute(buf_d, comb_d, c_d, first)
    hop_y = [
        send(part(c_d, first + i * piece, piece), part(via_y, i * piece, piece), y_dev)
        for i in range(4)
    ]
    tok_d1.wait_recv()
    compute(buf_d, comb_d, c_d, second)
    hop_x = [
        send(part(c_d, second + i * piece, piece), part(via_x, i * piece, piece), x_dev)
        for i in range(4)
    ]
    mid = half // 2
    straight.append(send(part(c_x, second + mid, mid), part(got_x, second + mid, mid), x_dev))
    straight.append(send(part(c_y, first + mid, mid), part(got_y, first + mid, mid), y_dev))

    def add(dst, dst_start, *terms):
        total = terms[0][0][pl.ds(terms[0][1], piece), :].astype(jnp.float32)
        for ref, start in terms[1:]:
            total = total + ref[pl.ds(start, piece), :].astype(jnp.float32)
        dst[pl.ds(dst_start, piece), :] = total.astype(jnp.bfloat16)

    last_x, last_y = [], []
    for i in range(4):
        at0, at1 = first + i * piece, second + i * piece
        hop_y[i].wait_recv()
        add(c_x, at0, (c_x, at0), (via_y, i * piece))
        last_x.append(send(part(c_x, at0, piece), part(got_x, at0, piece), x_dev))
        hop_x[i].wait_recv()
        add(c_y, at1, (c_y, at1), (via_x, i * piece))
        last_y.append(send(part(c_y, at1, piece), part(got_y, at1, piece), y_dev))

    for copy in straight:
        copy.wait_recv()
    for i in range(4):
        at0, at1 = first + i * piece, second + i * piece
        last_x[i].wait_recv()
        add(out_ref, at0, (c_own, at0), (got_x, at0), (got_y, at0))
        last_y[i].wait_recv()
        add(out_ref, at1, (c_own, at1), (got_x, at1), (got_y, at1))
    for copy in sent:
        copy.wait_send()


COPIES = 29


def local_square(tokens, routes, gate_values, weight_in, weight_out):
    rows, width = tokens.shape
    w_first, w_second = weight_in[0], weight_out[0]
    units = w_second.shape[0]
    block = pltpu.VMEM((rows, width), jnp.bfloat16)
    comb = pltpu.VMEM((16, rows), jnp.bfloat16)
    half_block = pltpu.VMEM((rows // 2, width), jnp.bfloat16)
    in_vmem = pl.BlockSpec(memory_space=pltpu.VMEM)
    anywhere = pl.BlockSpec(memory_space=pl.ANY)
    return pl.pallas_call(
        square_kernel,
        out_shape=jax.ShapeDtypeStruct((rows, width), jnp.bfloat16),
        in_specs=[in_vmem, in_vmem, anywhere, anywhere, anywhere],
        out_specs=in_vmem,
        scratch_shapes=[
            pltpu.VMEM(w_first.shape, jnp.bfloat16),
            pltpu.VMEM(w_second.shape, jnp.bfloat16),
            block, block, block, block,
            comb, comb, comb, comb,
            block, block, block, block,
            block, block,
            half_block, half_block,
            pltpu.VMEM((rows // 2, units), jnp.bfloat16),
            pltpu.SemaphoreType.DMA((3,)),
            pltpu.SemaphoreType.DMA((COPIES,)),
            pltpu.SemaphoreType.DMA((COPIES,)),
        ],
        compiler_params=pltpu.CompilerParams(
            collective_id=0, has_side_effects=True, vmem_limit_bytes=60 * 1024 * 1024
        ),
        cost_estimate=pl.CostEstimate(
            flops=4 * rows * width * units * 6, bytes_accessed=16 << 20, transcendentals=0
        ),
    )(routes.T, gate_values.T, tokens, w_first, w_second)


def local_dense(tokens, routes, gate_values, weight_in, weight_out):
    my_expert = lax.axis_index("expert")
    w_first, w_second = weight_in[0], weight_out[0]
    units = w_second.shape[0]
    experts = jnp.arange(lax.axis_size("expert"), dtype=jnp.int32)[None, None, :]
    matched = routes[:, :, None] == experts
    combine = jnp.sum(jnp.where(matched, gate_values.astype(jnp.float32)[:, :, None], 0.0), axis=1)
    gathered = lax.all_gather(tokens, "expert", axis=0, tiled=True)
    combine = lax.all_gather(combine, "expert", axis=0, tiled=True)
    mine = (experts[0] == my_expert).astype(jnp.float32)
    weight = jnp.sum(combine * mine, axis=1)
    projected = jnp.dot(gathered, w_first, preferred_element_type=jnp.float32)
    hidden = (jax.nn.silu(projected[:, :units]) * projected[:, units:]).astype(jnp.bfloat16)
    expert_out = jnp.dot(hidden, w_second, preferred_element_type=jnp.float32)
    contribution = (expert_out * weight[:, None]).astype(jnp.bfloat16)
    return lax.psum_scatter(contribution, "expert", scatter_dimension=0, tiled=True)


def solution(mesh):
    in_specs = (
        P(("dp", "expert"), None),
        P(("dp", "expert"), None),
        P(("dp", "expert"), None),
        P("expert", None, None),
        P("expert", None, None),
    )
    out_specs = P(("dp", "expert"), None)
    body = local_square if mesh.shape["expert"] == 4 else local_dense
    return jax.shard_map(body, mesh=mesh, in_specs=in_specs, out_specs=out_specs, check_vma=False)
```

```python
import jax
import jax.numpy as jnp
from jax import lax
from jax.experimental import pallas as pl
from jax.experimental.pallas import tpu as pltpu
from jax.sharding import PartitionSpec as P

MESH = pl.DeviceIdType.MESH


def square_kernel(
    routes_hbm, gates_hbm, tokens_ref, w_in_ref, w_out_ref, out_ref,
    routes_ref, gates_ref, w1, w2, own, buf_x, buf_y, buf_d, comb_own, comb_x, comb_y, comb_d,
    c_own, c_x, c_y, c_d, got_x, got_y, via_y, via_x, hidden,
    local_sem, send_sem, recv_sem,
):
    me = lax.axis_index("expert")
    x_dev = me + 1 - 2 * (me % 2)
    y_dev = (me + 2) % 4
    rows, width = own.shape
    half = rows // 2
    units = w2.shape[0]
    first, second = 0, half
    piece = half // 4

    barrier = pltpu.get_barrier_semaphore()
    for dev in (x_dev, y_dev):
        pl.semaphore_signal(barrier, inc=1, device_id={"expert": dev}, device_id_type=MESH)

    load_w1 = pltpu.make_async_copy(w_in_ref, w1, local_sem.at[0])
    load_w2 = pltpu.make_async_copy(w_out_ref, w2, local_sem.at[1])
    load_own = pltpu.make_async_copy(tokens_ref, own, local_sem.at[2])
    load_routes = pltpu.make_async_copy(routes_hbm, routes_ref, local_sem.at[3])
    load_gates = pltpu.make_async_copy(gates_hbm, gates_ref, local_sem.at[4])
    load_routes.start()
    load_gates.start()
    pl.semaphore_wait(barrier, 2)

    count = [0]
    sent = []

    def send(src, dst, dev):
        k = count[0]
        count[0] += 1
        copy = pltpu.make_async_remote_copy(
            src_ref=src,
            dst_ref=dst,
            send_sem=send_sem.at[k],
            recv_sem=recv_sem.at[k],
            device_id={"expert": dev},
            device_id_type=MESH,
        )
        copy.start()
        sent.append(copy)
        return copy

    def part(ref, start, size):
        return ref.at[pl.ds(start, size)]

    tok_x0 = send(part(tokens_ref, first, half), part(buf_x, first, half), x_dev)
    tok_y1 = send(part(tokens_ref, second, half), part(buf_y, second, half), y_dev)
    load_own.start()
    load_w1.start()
    load_w2.start()

    load_routes.wait()
    load_gates.wait()
    experts = lax.broadcasted_iota(jnp.int32, comb_own.shape, 0)
    combined = jnp.zeros(comb_own.shape, jnp.float32)
    for j in range(routes_ref.shape[0]):
        combined += jnp.where(
            experts == routes_ref[j : j + 1, :], gates_ref[j : j + 1, :].astype(jnp.float32), 0.0
        )
    comb_own[...] = combined.astype(jnp.bfloat16)
    com_x = send(comb_own, comb_x, x_dev)
    com_y = send(comb_own, comb_y, y_dev)

    tile = 256

    def compute(src, comb, dst, start):
        def first_step(j, carry):
            cols = pl.multiple_of(j * tile, tile)
            x = src[pl.ds(start, half), :]
            gate = jnp.dot(x, w1[:, pl.ds(cols, tile)], preferred_element_type=jnp.float32)
            up = jnp.dot(x, w1[:, pl.ds(cols + units, tile)], preferred_element_type=jnp.float32)
            hidden[:, pl.ds(cols, tile)] = (gate / (1.0 + jnp.exp(-gate)) * up).astype(jnp.bfloat16)
            return carry

        lax.fori_loop(0, units // tile, first_step, 0)
        pick = (lax.broadcasted_iota(jnp.int32, (comb.shape[0], 128), 0) == me).astype(jnp.bfloat16)
        weight = lax.dot_general(
            comb[:, pl.ds(start, half)], pick, (((0,), (0,)), ((), ())),
            preferred_element_type=jnp.float32,
        )[:, :1]

        def second_step(j, carry):
            cols = pl.multiple_of(j * 512, 512)
            got = jnp.dot(
                hidden[...], w2[:, pl.ds(cols, 512)], preferred_element_type=jnp.float32
            )
            dst[pl.ds(start, half), pl.ds(cols, 512)] = (got * weight).astype(jnp.bfloat16)
            return carry

        lax.fori_loop(0, width // 512, second_step, 0)

    load_own.wait()
    load_w1.wait()
    load_w2.wait()
    compute(own, comb_own, c_own, first)
    tok_x1 = send(part(tokens_ref, second, half), part(buf_x, second, half), x_dev)
    tok_y0 = send(part(tokens_ref, first, half), part(buf_y, first, half), y_dev)
    compute(own, comb_own, c_own, second)

    com_x.wait_recv()
    com_y.wait_recv()
    com_d = send(comb_x, comb_d, y_dev)
    tok_x0.wait_recv()
    tok_d0 = send(part(buf_x, first, half), part(buf_d, first, half), y_dev)
    tok_y1.wait_recv()
    tok_d1 = send(part(buf_y, second, half), part(buf_d, second, half), x_dev)
    compute(buf_x, comb_x, c_x, first)
    compute(buf_y, comb_y, c_y, second)

    tok_x1.wait_recv()
    straight_x = send(part(c_x, first, half), part(got_x, first, half), x_dev)
    tok_y0.wait_recv()
    straight_y = send(part(c_y, second, half), part(got_y, second, half), y_dev)
    compute(buf_x, comb_x, c_x, second)
    compute(buf_y, comb_y, c_y, first)

    com_d.wait_recv()
    tok_d0.wait_recv()
    compute(buf_d, comb_d, c_d, first)
    hop_x = [
        send(part(c_d, first + i * piece, piece), part(via_x, i * piece, piece), x_dev)
        for i in range(4)
    ]
    tok_d1.wait_recv()
    compute(buf_d, comb_d, c_d, second)
    hop_y = [
        send(part(c_d, second + i * piece, piece), part(via_y, i * piece, piece), y_dev)
        for i in range(4)
    ]

    def add(dst, dst_start, *terms):
        total = terms[0][0][pl.ds(terms[0][1], piece), :].astype(jnp.float32)
        for ref, start in terms[1:]:
            total = total + ref[pl.ds(start, piece), :].astype(jnp.float32)
        dst[pl.ds(dst_start, piece), :] = total.astype(jnp.bfloat16)

    last_x, last_y = [], []
    for i in range(4):
        at0, at1 = first + i * piece, second + i * piece
        hop_x[i].wait_recv()
        add(c_y, at0, (c_y, at0), (via_x, i * piece))
        last_y.append(send(part(c_y, at0, piece), part(got_y, at0, piece), y_dev))
        hop_y[i].wait_recv()
        add(c_x, at1, (c_x, at1), (via_y, i * piece))
        last_x.append(send(part(c_x, at1, piece), part(got_x, at1, piece), x_dev))

    straight_x.wait_recv()
    straight_y.wait_recv()
    for i in range(4):
        at0, at1 = first + i * piece, second + i * piece
        last_y[i].wait_recv()
        add(out_ref, at0, (c_own, at0), (got_x, at0), (got_y, at0))
        last_x[i].wait_recv()
        add(out_ref, at1, (c_own, at1), (got_x, at1), (got_y, at1))
    for copy in sent:
        copy.wait_send()


COPIES = 27


def local_square(tokens, routes, gate_values, weight_in, weight_out):
    rows, width = tokens.shape
    w_first, w_second = weight_in[0], weight_out[0]
    units = w_second.shape[0]
    block = pltpu.VMEM((rows, width), jnp.bfloat16)
    comb = pltpu.VMEM((16, rows), jnp.bfloat16)
    half_block = pltpu.VMEM((rows // 2, width), jnp.bfloat16)
    in_vmem = pl.BlockSpec(memory_space=pltpu.VMEM)
    anywhere = pl.BlockSpec(memory_space=pl.ANY)
    return pl.pallas_call(
        square_kernel,
        out_shape=jax.ShapeDtypeStruct((rows, width), jnp.bfloat16),
        in_specs=[anywhere, anywhere, anywhere, anywhere, anywhere],
        out_specs=in_vmem,
        scratch_shapes=[
            pltpu.VMEM((routes.shape[1], rows), jnp.int32),
            pltpu.VMEM((routes.shape[1], rows), jnp.bfloat16),
            pltpu.VMEM(w_first.shape, jnp.bfloat16),
            pltpu.VMEM(w_second.shape, jnp.bfloat16),
            block, block, block, block,
            comb, comb, comb, comb,
            block, block, block, block,
            block, block,
            half_block, half_block,
            pltpu.VMEM((rows // 2, units), jnp.bfloat16),
            pltpu.SemaphoreType.DMA((5,)),
            pltpu.SemaphoreType.DMA((COPIES,)),
            pltpu.SemaphoreType.DMA((COPIES,)),
        ],
        compiler_params=pltpu.CompilerParams(
            collective_id=0, has_side_effects=True, vmem_limit_bytes=60 * 1024 * 1024
        ),
        cost_estimate=pl.CostEstimate(
            flops=4 * rows * width * units * 6, bytes_accessed=16 << 20, transcendentals=0
        ),
    )(routes.T, gate_values.T, tokens, w_first, w_second)


def local_dense(tokens, routes, gate_values, weight_in, weight_out):
    my_expert = lax.axis_index("expert")
    w_first, w_second = weight_in[0], weight_out[0]
    units = w_second.shape[0]
    experts = jnp.arange(lax.axis_size("expert"), dtype=jnp.int32)[None, None, :]
    matched = routes[:, :, None] == experts
    combine = jnp.sum(jnp.where(matched, gate_values.astype(jnp.float32)[:, :, None], 0.0), axis=1)
    gathered = lax.all_gather(tokens, "expert", axis=0, tiled=True)
    combine = lax.all_gather(combine, "expert", axis=0, tiled=True)
    mine = (experts[0] == my_expert).astype(jnp.float32)
    weight = jnp.sum(combine * mine, axis=1)
    projected = jnp.dot(gathered, w_first, preferred_element_type=jnp.float32)
    hidden = (jax.nn.silu(projected[:, :units]) * projected[:, units:]).astype(jnp.bfloat16)
    expert_out = jnp.dot(hidden, w_second, preferred_element_type=jnp.float32)
    contribution = (expert_out * weight[:, None]).astype(jnp.bfloat16)
    return lax.psum_scatter(contribution, "expert", scatter_dimension=0, tiled=True)


def solution(mesh):
    in_specs = (
        P(("dp", "expert"), None),
        P(("dp", "expert"), None),
        P(("dp", "expert"), None),
        P("expert", None, None),
        P("expert", None, None),
    )
    out_specs = P(("dp", "expert"), None)
    body = local_square if mesh.shape["expert"] == 4 else local_dense
    return jax.shard_map(body, mesh=mesh, in_specs=in_specs, out_specs=out_specs, check_vma=False)
```

```python
import jax
import jax.numpy as jnp
from jax import lax
from jax.experimental import pallas as pl
from jax.experimental.pallas import tpu as pltpu
from jax.sharding import PartitionSpec as P

MESH = pl.DeviceIdType.MESH


def square_kernel(
    routes_hbm, gates_hbm, tokens_ref, w_in_ref, w_out_ref, out_ref,
    routes_ref, gates_ref, w1, w2, own, buf_x, buf_y, buf_d, comb_own, comb_x, comb_y, comb_d,
    c_own, c_x, c_y, c_d, got_x, got_y, via_y, via_x, hidden,
    local_sem, send_sem, recv_sem,
):
    me = lax.axis_index("expert")
    x_dev = me + 1 - 2 * (me % 2)
    y_dev = (me + 2) % 4
    rows, width = own.shape
    half = rows // 2
    units = w2.shape[0]
    first, second = 0, half
    piece = half // 4

    barrier = pltpu.get_barrier_semaphore()
    for dev in (x_dev, y_dev):
        pl.semaphore_signal(barrier, inc=1, device_id={"expert": dev}, device_id_type=MESH)

    load_w1 = pltpu.make_async_copy(w_in_ref, w1, local_sem.at[0])
    load_w2 = pltpu.make_async_copy(w_out_ref, w2, local_sem.at[1])
    load_own = pltpu.make_async_copy(tokens_ref, own, local_sem.at[2])
    load_routes = pltpu.make_async_copy(routes_hbm, routes_ref, local_sem.at[3])
    load_gates = pltpu.make_async_copy(gates_hbm, gates_ref, local_sem.at[4])
    load_routes.start()
    load_gates.start()
    pl.semaphore_wait(barrier, 2)

    count = [0]
    sent = []

    def send(src, dst, dev):
        k = count[0]
        count[0] += 1
        copy = pltpu.make_async_remote_copy(
            src_ref=src,
            dst_ref=dst,
            send_sem=send_sem.at[k],
            recv_sem=recv_sem.at[k],
            device_id={"expert": dev},
            device_id_type=MESH,
        )
        copy.start()
        sent.append(copy)
        return copy

    def part(ref, start, size):
        return ref.at[pl.ds(start, size)]

    tok_x0 = send(part(tokens_ref, first, half), part(buf_x, first, half), x_dev)
    tok_y1 = send(part(tokens_ref, second, half), part(buf_y, second, half), y_dev)
    load_own.start()
    load_w1.start()
    load_w2.start()

    load_routes.wait()
    load_gates.wait()
    experts = lax.broadcasted_iota(jnp.int32, comb_own.shape, 0)
    combined = jnp.zeros(comb_own.shape, jnp.float32)
    for j in range(routes_ref.shape[0]):
        combined += jnp.where(
            experts == routes_ref[j : j + 1, :], gates_ref[j : j + 1, :].astype(jnp.float32), 0.0
        )
    comb_own[...] = combined.astype(jnp.bfloat16)
    com_x = send(comb_own, comb_x, x_dev)
    com_y = send(comb_own, comb_y, y_dev)

    tile = 256

    def compute(src, comb, dst, start):
        def first_step(j, carry):
            cols = pl.multiple_of(j * tile, tile)
            x = src[pl.ds(start, half), :]
            gate = jnp.dot(x, w1[:, pl.ds(cols, tile)], preferred_element_type=jnp.float32)
            up = jnp.dot(x, w1[:, pl.ds(cols + units, tile)], preferred_element_type=jnp.float32)
            hidden[:, pl.ds(cols, tile)] = (gate / (1.0 + jnp.exp(-gate)) * up).astype(jnp.bfloat16)
            return carry

        lax.fori_loop(0, units // tile, first_step, 0)
        pick = (lax.broadcasted_iota(jnp.int32, (comb.shape[0], 128), 0) == me).astype(jnp.bfloat16)
        weight = lax.dot_general(
            comb[:, pl.ds(start, half)], pick, (((0,), (0,)), ((), ())),
            preferred_element_type=jnp.float32,
        )[:, :1]

        def second_step(j, carry):
            cols = pl.multiple_of(j * 512, 512)
            got = jnp.dot(
                hidden[...], w2[:, pl.ds(cols, 512)], preferred_element_type=jnp.float32
            )
            dst[pl.ds(start, half), pl.ds(cols, 512)] = (got * weight).astype(jnp.bfloat16)
            return carry

        lax.fori_loop(0, width // 512, second_step, 0)

    load_own.wait()
    load_w1.wait()
    load_w2.wait()
    compute(own, comb_own, c_own, first)
    tok_x1 = send(part(tokens_ref, second, half), part(buf_x, second, half), x_dev)
    tok_y0 = send(part(tokens_ref, first, half), part(buf_y, first, half), y_dev)
    compute(own, comb_own, c_own, second)

    com_x.wait_recv()
    com_y.wait_recv()
    com_d = send(comb_x, comb_d, y_dev)
    tok_x0.wait_recv()
    tok_d0 = send(part(buf_x, first, half), part(buf_d, first, half), y_dev)
    tok_y1.wait_recv()
    tok_d1 = send(part(buf_y, second, half), part(buf_d, second, half), x_dev)
    compute(buf_x, comb_x, c_x, first)
    compute(buf_y, comb_y, c_y, second)

    tok_x1.wait_recv()
    straight_x = send(part(c_x, first, half), part(got_x, first, half), x_dev)
    tok_y0.wait_recv()
    straight_y = send(part(c_y, second, half), part(got_y, second, half), y_dev)
    compute(buf_x, comb_x, c_x, second)
    compute(buf_y, comb_y, c_y, first)

    com_d.wait_recv()
    tok_d0.wait_recv()
    compute(buf_d, comb_d, c_d, first)
    hop_x = [
        send(part(c_d, first + i * piece, piece), part(via_x, i * piece, piece), x_dev)
        for i in range(4)
    ]
    tok_d1.wait_recv()
    compute(buf_d, comb_d, c_d, second)
    hop_y = [
        send(part(c_d, second + i * piece, piece), part(via_y, i * piece, piece), y_dev)
        for i in range(4)
    ]

    def add(dst, dst_start, *terms):
        total = terms[0][0][pl.ds(terms[0][1], piece), :].astype(jnp.float32)
        for ref, start in terms[1:]:
            total = total + ref[pl.ds(start, piece), :].astype(jnp.float32)
        dst[pl.ds(dst_start, piece), :] = total.astype(jnp.bfloat16)

    last_x, last_y = [], []
    for i in range(4):
        at0, at1 = first + i * piece, second + i * piece
        hop_x[i].wait_recv()
        add(c_y, at0, (c_y, at0), (via_x, i * piece))
        last_y.append(send(part(c_y, at0, piece), part(got_y, at0, piece), y_dev))
        hop_y[i].wait_recv()
        add(c_x, at1, (c_x, at1), (via_y, i * piece))
        last_x.append(send(part(c_x, at1, piece), part(got_x, at1, piece), x_dev))

    straight_x.wait_recv()
    straight_y.wait_recv()
    for i in range(4):
        at0, at1 = first + i * piece, second + i * piece
        last_y[i].wait_recv()
        add(out_ref, at0, (c_own, at0), (got_x, at0), (got_y, at0))
        last_x[i].wait_recv()
        add(out_ref, at1, (c_own, at1), (got_x, at1), (got_y, at1))
    for copy in sent:
        copy.wait_send()


COPIES = 27


def local_square(tokens, routes, gate_values, weight_in, weight_out):
    rows, width = tokens.shape
    w_first, w_second = weight_in[0], weight_out[0]
    units = w_second.shape[0]
    block = pltpu.VMEM((rows, width), jnp.bfloat16)
    comb = pltpu.VMEM((16, rows), jnp.bfloat16)
    half_block = pltpu.VMEM((rows // 2, width), jnp.bfloat16)
    in_vmem = pl.BlockSpec(memory_space=pltpu.VMEM)
    anywhere = pl.BlockSpec(memory_space=pl.ANY)
    return pl.pallas_call(
        square_kernel,
        out_shape=jax.ShapeDtypeStruct((rows, width), jnp.bfloat16),
        in_specs=[anywhere, anywhere, anywhere, anywhere, anywhere],
        out_specs=in_vmem,
        scratch_shapes=[
            pltpu.VMEM((routes.shape[1], rows), jnp.int32),
            pltpu.VMEM((routes.shape[1], rows), jnp.bfloat16),
            pltpu.VMEM(w_first.shape, jnp.bfloat16),
            pltpu.VMEM(w_second.shape, jnp.bfloat16),
            block, block, block, block,
            comb, comb, comb, comb,
            block, block, block, block,
            block, block,
            half_block, half_block,
            pltpu.VMEM((rows // 2, units), jnp.bfloat16),
            pltpu.SemaphoreType.DMA((5,)),
            pltpu.SemaphoreType.DMA((COPIES,)),
            pltpu.SemaphoreType.DMA((COPIES,)),
        ],
        compiler_params=pltpu.CompilerParams(
            collective_id=0, has_side_effects=True, vmem_limit_bytes=52 * 1024 * 1024
        ),
        cost_estimate=pl.CostEstimate(
            flops=4 * rows * width * units * 6, bytes_accessed=16 << 20, transcendentals=0
        ),
    )(routes.T, gate_values.T, tokens, w_first, w_second)


def local_dense(tokens, routes, gate_values, weight_in, weight_out):
    my_expert = lax.axis_index("expert")
    w_first, w_second = weight_in[0], weight_out[0]
    units = w_second.shape[0]
    experts = jnp.arange(lax.axis_size("expert"), dtype=jnp.int32)[None, None, :]
    matched = routes[:, :, None] == experts
    combine = jnp.sum(jnp.where(matched, gate_values.astype(jnp.float32)[:, :, None], 0.0), axis=1)
    gathered = lax.all_gather(tokens, "expert", axis=0, tiled=True)
    combine = lax.all_gather(combine, "expert", axis=0, tiled=True)
    mine = (experts[0] == my_expert).astype(jnp.float32)
    weight = jnp.sum(combine * mine, axis=1)
    projected = jnp.dot(gathered, w_first, preferred_element_type=jnp.float32)
    hidden = (jax.nn.silu(projected[:, :units]) * projected[:, units:]).astype(jnp.bfloat16)
    expert_out = jnp.dot(hidden, w_second, preferred_element_type=jnp.float32)
    contribution = (expert_out * weight[:, None]).astype(jnp.bfloat16)
    return lax.psum_scatter(contribution, "expert", scatter_dimension=0, tiled=True)


def solution(mesh):
    in_specs = (
        P(("dp", "expert"), None),
        P(("dp", "expert"), None),
        P(("dp", "expert"), None),
        P("expert", None, None),
        P("expert", None, None),
    )
    out_specs = P(("dp", "expert"), None)
    body = local_square if mesh.shape["expert"] == 4 else local_dense
    return jax.shard_map(body, mesh=mesh, in_specs=in_specs, out_specs=out_specs, check_vma=False)
```
